512 devices in a mesh: leaf: 4 (over z_hi), row: 8 (over y), col: 16 (over z_lo, x, core).
Axes of the slice: x: 4, y: 8, z: 8 (z_hi: 4, z_lo: 2; z = z_hi * 2 + z_lo), core: 2. Of those that a mesh axis runs over, the one named last changes fastest.
Arguments:
- y_root: bfloat16 [16384, 256], P('col', ('leaf', 'row')), may hold values from -6 to 6
- root_inverse: bfloat16 [16384, 16384], P(('leaf', 'row'), 'col'), may hold values from -0.046875 to 0.046875
- block_map: int32 [4, 16], replicated, may hold values from 0 to 63, as said below
- y_child: bfloat16 [4, 12288, 256], P('leaf', 'row'), may hold values from -6 to 6
- panel: bfloat16 [4, 12288, 4096], P('leaf', 'row', 'col'), may hold values from -0.09375 to 0.09375
- child_inverse: bfloat16 [4, 12288, 12288], P('leaf', 'row', 'col'), may hold values from -0.0546875 to 0.0546875
Outputs:
- x_root: bfloat16 [16384, 256], P(('leaf', 'row', 'col'))
- x_child: bfloat16 [4, 12288, 256], P('leaf', ('row', 'col'))
The draws below stay inside these ranges and needn't reach their ends.
Inputs may be any that keep to these rules, and one draw needn't show every extreme that they name: `block_map`: each of the 16384 // 256 root blocks appears exactly once in the whole map; the blocks of child k are all those of root rows g * 4096 to (g + 1) * 4096 - 1 for one group g, which is k or (k + 2) % 4, in an order drawn from the seed.
All inputs are finite; a program needn't handle non-finite values.
Results may differ from the reference program's by a relative error of at most 0.018.
Values may be sent and summed in bfloat16 or wider, within the bound.
A program may use at most 64 MiB of HBM per device.

```python
import jax
import jax.numpy as jnp

R = 16384
S = 12288
BLK = 256
NRHS = 256
CHILDREN = 4
U = 4096


def draw_block_map(key, part):
    key = jax.random.fold_in(key, 11)
    flip_key, order_key = jax.random.split(key)
    half_count = CHILDREN // 2
    per_group = U // BLK
    offset = jax.random.randint(flip_key, (), 0, 2, dtype=jnp.int32)
    kids = jnp.arange(CHILDREN, dtype=jnp.int32)
    flipped = (kids % half_count + offset) % 2
    source = (kids + half_count * flipped) % CHILDREN
    orders = jax.vmap(lambda sub: jax.random.permutation(sub, per_group))(jax.random.split(order_key, CHILDREN))
    return (source[:, None] * per_group + orders.astype(jnp.int32)).astype(jnp.int32)


def level_of(rng, extent, cuts, least, high):
    factor_of = 1.0
    for axis_at, parts in cuts:
        draws = jax.random.uniform(jax.random.fold_in(jax.random.fold_in(rng, 6), axis_at), (parts,), jnp.float32, least / len(cuts), high / len(cuts))
        factor_of = factor_of * jnp.repeat(jnp.exp(draws), extent[axis_at] // parts).reshape((-1,) + (1,) * (len(extent) - 1 - axis_at))
    return factor_of


def bell_draw(stream_key, shape, width, most, cuts=(), kind=jnp.bfloat16):
    level = level_of(stream_key, shape, cuts, -0.22, 0.18) if cuts else 1.0
    result = jax.random.normal(stream_key, shape, jnp.float32) * width * level
    return jnp.minimum(jnp.maximum(result, -most), most).astype(kind)


def setup_inputs(seed: int = 0) -> dict:
    key_of = jax.random.split(jax.random.key(seed), 7)
    return {
        "y_root": bell_draw(key_of[0], (R, NRHS), 1.0, 6.0, ((0, 16), (1, 32))),
        "root_inverse": bell_draw(key_of[1], (R, R), R ** -0.5, 0.046875, ((0, 32), (1, 16))),
        "block_map": draw_block_map(jax.random.fold_in(key_of[6], 71), 0),
        "y_child": bell_draw(key_of[3], (CHILDREN, S, NRHS), 1.0, 6.0, ((0, 4), (1, 8))),
        "panel": bell_draw(key_of[4], (CHILDREN, S, U), U ** -0.5, 0.09375, ((0, 4), (1, 8), (2, 16))),
        "child_inverse": bell_draw(key_of[5], (CHILDREN, S, S), S ** -0.5, 0.0546875, ((0, 4), (1, 8), (2, 16))),
    }


def reference(y_root, root_inverse, block_map, y_child, panel, child_inverse):
    x_root = jnp.dot(root_inverse, y_root, preferred_element_type=jnp.float32).astype(jnp.bfloat16)
    row_index_map = (block_map[:, :, None] * BLK + jnp.arange(BLK, dtype=jnp.int32)[None, None, :]).reshape(CHILDREN, U).astype(jnp.int32)
    results = []
    for child_index in range(CHILDREN):
        selected = jnp.take(x_root, row_index_map[child_index], axis=0)
        update = jnp.dot(panel[child_index], selected, preferred_element_type=jnp.float32)
        reduced = (y_child[child_index].astype(jnp.float32) - update).astype(jnp.bfloat16)
        results.append(jnp.dot(child_inverse[child_index], reduced, preferred_element_type=jnp.float32).astype(jnp.bfloat16))
    return x_root, jnp.stack(results)
```

```python
import jax
import jax.numpy as jnp
from jax import lax
from jax.experimental import pallas as pl
from jax.experimental.pallas import tpu as pltpu
from jax.sharding import PartitionSpec as P

MESH = pl.DeviceIdType.MESH
BF, F32 = jnp.bfloat16, jnp.float32

LEAF, ROW, COL, CHIP = 4, 8, 16, 8
NH = 2
W = 256 // NH
LH = LEAF // NH

DMA = pltpu.SemaphoreType.DMA
SCRATCH = dict(
    inv_v=pltpu.VMEM((512, 1024), BF),
    panel_v=pltpu.VMEM((2, 768, 256), BF),
    cinv_v=pltpu.VMEM((2, 8, 96, 768), BF),
    yc_v=pltpu.VMEM((96, 256), BF),
    load=DMA((5,)),
    ybuf=pltpu.VMEM((LEAF, ROW, 16, 512), BF),
    z_s=DMA((3,)),
    z_r=DMA((3,)),
    ring_s=DMA((NH, 2, 4)),
    ring_r=DMA((NH, 2, 4)),
    xpart=pltpu.VMEM((NH, COL, 2, 16, W), BF),
    xin=pltpu.VMEM((NH, COL - 1, 2, 16, W), BF),
    xin_s=DMA((NH, COL - 1)),
    xin_r=DMA((NH, COL - 1)),
    **{f"xpair{h}": pltpu.VMEM((2, 2, 16, W), BF) for h in range(NH)},
    swap_s=DMA((NH,)),
    swap_r=DMA((NH,)),
    **{f"xg{h}": pltpu.VMEM((16, 16, W), BF) for h in range(NH)},
    xg_s=DMA((NH, ROW - 1)),
    xg_r=DMA((NH, ROW - 1)),
    picked=pltpu.VMEM((NH, COL - 1, 16, W), BF),
    sel=pltpu.VMEM((NH, COL, 16, W), BF),
    sel_s=DMA((NH, COL - 1)),
    sel_r=DMA((NH, COL - 1)),
    xo=pltpu.VMEM((2, NH, 16, W), BF),
    xo_s=DMA((NH, 2)),
    xo_r=DMA((NH, 2)),
    pother=pltpu.VMEM((NH, 8, 96, W), BF),
    pin=pltpu.VMEM((NH, 8, 96, W), BF),
    pin_s=DMA((NH,)),
    pin_r=DMA((NH,)),
    pown=pltpu.VMEM((NH, 8, 96, W), F32),
    pout=pltpu.VMEM((NH, CHIP - 1, 96, W), BF),
    prx=pltpu.VMEM((NH, CHIP - 1, 96, W), BF),
    prx_s=DMA((NH, CHIP - 1)),
    prx_r=DMA((NH, CHIP - 1)),
    red=pltpu.VMEM((NH, 96, W), BF),
    turn_s=DMA((NH,)),
    turn_r=DMA((NH,)),
    rf=pltpu.VMEM((NH, ROW, 96, W), BF),
    rf_s=DMA((NH, ROW - 1)),
    rf_r=DMA((NH, ROW - 1)),
    cother=pltpu.VMEM((NH, 8, 96, W), BF),
    cin=pltpu.VMEM((NH, 8, 96, W), BF),
    cin_s=DMA((NH,)),
    cin_r=DMA((NH,)),
    cown=pltpu.VMEM((NH, 8, 96, W), F32),
    cout=pltpu.VMEM((NH, CHIP - 1, 96, W), BF),
    crx=pltpu.VMEM((NH, CHIP - 1, 96, W), BF),
    crx_s=DMA((NH, CHIP - 1)),
    crx_r=DMA((NH, CHIP - 1)),
)


class Refs:
    pass


def kernel(y_ref, inv_ref, map_ref, yc_ref, panel_ref, cinv_ref, xroot_ref, xchild_ref, *scratch):
    k = Refs()
    for name, ref in zip(SCRATCH, scratch):
        setattr(k, name, ref)
    xpair = [getattr(k, f"xpair{h}") for h in range(NH)]
    xg = [getattr(k, f"xg{h}") for h in range(NH)]
    leaf, row, col = lax.axis_index("leaf"), lax.axis_index("row"), lax.axis_index("col")
    core, chip = col % 2, col // 2
    sent = []

    def remote(src, dst, send, recv, device):
        return pltpu.make_async_remote_copy(
            src_ref=src, dst_ref=dst, send_sem=send, recv_sem=recv, device_id=device, device_id_type=MESH
        )

    def go(copy):
        copy.start()
        sent.append(copy)

    def leaf_peer(p):
        return ((leaf + p) % LEAF, row, col)

    def row_peer(p):
        return (leaf, (row + p) % ROW, col)

    def col_peer(p):
        return (leaf, row, (col + p) % COL)

    def chip_peer(p):
        return (leaf, row, 2 * ((chip + p) % CHIP) + core)

    twin = (leaf, row, col + 1 - 2 * core)
    turned = (leaf, chip, 2 * row + core)

    loads = [
        pltpu.make_async_copy(inv_ref, k.inv_v, k.load.at[0]),
        pltpu.make_async_copy(panel_ref, k.panel_v, k.load.at[1]),
        pltpu.make_async_copy(yc_ref.at[8 * core + chip], k.yc_v, k.load.at[2]),
        pltpu.make_async_copy(cinv_ref.at[:, 0], k.cinv_v.at[0], k.load.at[3]),
        pltpu.make_async_copy(cinv_ref.at[:, 1], k.cinv_v.at[1], k.load.at[4]),
    ]
    for load in loads:
        load.start()

    barrier = pltpu.get_barrier_semaphore()

    def greet(device):
        pl.semaphore_signal(barrier, inc=1, device_id=device, device_id_type=MESH)

    for p in range(1, LEAF):
        greet(leaf_peer(p))
    for p in range(1, ROW):
        greet(row_peer(p))
    for p in range(1, COL):
        greet(col_peer(p))

    @pl.when(chip != row)
    def _():
        greet(turned)

    y = y_ref[...].astype(F32)
    k.ybuf[leaf, row] = jnp.concatenate([y[:, :512], y[:, 512:]], axis=0).astype(BF)

    pl.semaphore_wait(barrier, LEAF - 1 + ROW - 1 + COL - 1 + jnp.where(chip == row, 0, 1))

    exchange = []
    for p in range(1, LEAF):
        slot = k.ybuf.at[leaf, row]
        exchange.append(remote(slot, slot, k.z_s.at[p - 1], k.z_r.at[p - 1], leaf_peer(p)))
        go(exchange[-1])

    def ring_step(h, step):
        copies = []
        for way in range(2):
            at = (row - step + ROW) % ROW if way == 0 else (row + step) % ROW
            leaves = pl.ds(h * LH, LH) if step < 3 else pl.ds(h * LH + way * (LH // 2), LH // 2)
            part = k.ybuf.at[leaves, at]
            copies.append(
                remote(part, part, k.ring_s.at[h, way, step], k.ring_r.at[h, way, step], row_peer(1 if way == 0 else ROW - 1))
            )
        return copies

    for copy in exchange:
        copy.wait_recv()
    ring = {}
    for step in range(4):
        for h in range(NH):
            if step:
                for copy in ring[h]:
                    copy.wait_recv()
            ring[h] = ring_step(h, step)
            for copy in ring[h]:
                go(copy)

    flight = {}

    def send_all(name, h, copies):
        for copy in copies:
            go(copy)
        flight[name, h] = copies

    def arrived(name, h):
        for copy in flight.pop((name, h)):
            copy.wait_recv()

    def root_mm(h):
        if h == 0:
            loads[0].wait()
        for copy in ring.pop(h):
            copy.wait_recv()
        y = k.ybuf[h * LH : (h + 1) * LH].astype(F32)
        total = None
        for half in range(2):
            part = y[:, :, 8 * half : 8 * half + 8, :].reshape(W, 512).astype(BF)
            term = lax.dot_general(
                k.inv_v[:, 512 * half : 512 * half + 512],
                part,
                (((1,), (1,)), ((), ())),
                preferred_element_type=F32,
            )
            total = term if total is None else total + term
        total = total.astype(BF)
        for block in range(2):
            k.xpart[h, :, block] = total[256 * block : 256 * block + 256].reshape(COL, 16, W)
        send_all(
            "x",
            h,
            [
                remote(k.xpart.at[h, (col + p) % COL], k.xin.at[h, p - 1], k.xin_s.at[h, p - 1], k.xin_r.at[h, p - 1], col_peer(p))
                for p in range(1, COL)
            ],
        )

    def root_sum(h):
        arrived("x", h)
        total = k.xpart[h, col].astype(F32)
        for p in range(COL - 1):
            total = total + k.xin[h, p].astype(F32)
        xpair[h][0] = total.astype(BF)
        send_all("swap", h, [remote(xpair[h].at[0], xpair[h].at[1], k.swap_s.at[h], k.swap_r.at[h], leaf_peer(2))])
        root_out(h)

    def root_copy(h, block):
        target = 8 * block + col // 2
        return target, remote(
            xpair[h].at[0, block], k.xo.at[col % 2, h], k.xo_s.at[h, block], k.xo_r.at[h, col % 2], (leaf, row, target)
        )

    def root_out(h):
        for block in range(2):
            target, copy = root_copy(h, block)

            @pl.when(target != col)
            def _():
                copy.start()

            @pl.when(target == col)
            def _():
                k.xo[col % 2, h] = xpair[h][0, block]

    def root_finish(h):
        for block in range(2):
            target, copy = root_copy(h, block)

            @pl.when(target != col)
            def _():
                copy.wait_send()

        for slot in range(2):

            @pl.when(2 * (col % 8) + slot != col)
            def _():
                remote(xpair[h].at[0, 0], k.xo.at[slot, h], k.xo_s.at[h, 0], k.xo_r.at[h, slot], (leaf, row, col)).wait_recv()

            xroot_ref[16 * slot : 16 * slot + 16, h * W : (h + 1) * W] = k.xo[slot, h]

    def y_spread(h):
        arrived("swap", h)
        swapped = jnp.where(map_ref[leaf, 0] // 16 == leaf, 0, 1)
        mine = xg[h].at[pl.ds(2 * row, 2)]
        xg[h][pl.ds(2 * row, 2)] = xpair[h][swapped]
        send_all(
            "g",
            h,
            [remote(mine, mine, k.xg_s.at[h, p - 1], k.xg_r.at[h, p - 1], row_peer(p)) for p in range(1, ROW)],
        )

    def col_spread(h):
        arrived("g", h)
        copies = []
        for p in range(1, COL):
            k.picked[h, p - 1] = xg[h][map_ref[leaf, (col + p) % COL] % 16]
            copies.append(remote(k.picked.at[h, p - 1], k.sel.at[h, col], k.sel_s.at[h, p - 1], k.sel_r.at[h, p - 1], col_peer(p)))
            go(copies[-1])
        flight["sel", h] = copies
        k.sel[h, col] = xg[h][map_ref[leaf, col] % 16]

    def times(tile, right):
        return jnp.dot(tile, right, preferred_element_type=F32).reshape(8, 96, W)

    def panel_mm(h):
        if h == 0:
            loads[1].wait()
        arrived("sel", h)
        right = k.sel[h].reshape(256, W)
        k.pother[h] = times(k.panel_v[1 - core], right).astype(BF)
        send_all("pin", h, [remote(k.pother.at[h], k.pin.at[h], k.pin_s.at[h], k.pin_r.at[h], twin)])
        k.pown[h] = times(k.panel_v[core], right)

    def scatter(h, name, own, inc, out, rx, send, recv):
        copies = []
        for p in range(1, CHIP):
            at = (chip + p) % CHIP
            out[h, p - 1] = (own[h, at] + inc[h, at].astype(F32)).astype(BF)
            copies.append(remote(out.at[h, p - 1], rx.at[h, p - 1], send.at[h, p - 1], recv.at[h, p - 1], chip_peer(p)))
            go(copies[-1])
        flight[name, h] = copies

    def gathered(h, own, inc, rx):
        total = own[h, chip] + inc[h, chip].astype(F32)
        for p in range(CHIP - 1):
            total = total + rx[h, p].astype(F32)
        return total

    def panel_rs(h):
        arrived("pin", h)
        scatter(h, "prx", k.pown, k.pin, k.pout, k.prx, k.prx_s, k.prx_r)

    def turn(h):
        return remote(k.red.at[h], k.rf.at[h, chip], k.turn_s.at[h], k.turn_r.at[h], turned)

    def panel_sum(h):
        if h == 0:
            loads[2].wait()
        arrived("prx", h)
        yc = k.yc_v[:, h * W : (h + 1) * W].astype(F32)
        k.red[h] = (yc - gathered(h, k.pown, k.pin, k.prx)).astype(BF)

        @pl.when(chip != row)
        def _():
            turn(h).start()

        @pl.when(chip == row)
        def _():
            k.rf[h, row] = k.red[h]

    def slab_spread(h):
        @pl.when(chip != row)
        def _():
            turn(h).wait()

        mine = k.rf.at[h, row]
        send_all(
            "rf",
            h,
            [remote(mine, mine, k.rf_s.at[h, p - 1], k.rf_r.at[h, p - 1], row_peer(p)) for p in range(1, ROW)],
        )

    def child_mm(h):
        if h == 0:
            loads[3].wait()
            loads[4].wait()
        arrived("rf", h)
        right = k.rf[h].reshape(768, W)
        k.cother[h] = times(k.cinv_v[1 - core].reshape(768, 768), right).astype(BF)
        send_all("cin", h, [remote(k.cother.at[h], k.cin.at[h], k.cin_s.at[h], k.cin_r.at[h], twin)])
        k.cown[h] = times(k.cinv_v[core].reshape(768, 768), right)

    def child_rs(h):
        arrived("cin", h)
        scatter(h, "crx", k.cown, k.cin, k.cout, k.crx, k.crx_s, k.crx_r)

    def child_sum(h):
        arrived("crx", h)
        xchild_ref[:, h * W : (h + 1) * W] = gathered(h, k.cown, k.cin, k.crx).astype(BF)

    stages = [
        root_mm, root_sum, y_spread, col_spread, panel_mm, panel_rs,
        panel_sum, slab_spread, child_mm, child_rs, child_sum,
    ]
    for t in range(len(stages) + NH - 1):
        for h in range(NH):
            if 0 <= t - h < len(stages):
                stages[t - h](h)
    for h in range(NH):
        root_finish(h)
    for copy in sent:
        copy.wait_send()


def per_device(y_root, root_inverse, block_map, y_child, panel, child_inverse):
    vmem = pl.BlockSpec(memory_space=pltpu.VMEM)
    hbm = pl.BlockSpec(memory_space=pl.ANY)
    x_root, x_child = pl.pallas_call(
        kernel,
        out_shape=(jax.ShapeDtypeStruct((32, 256), BF), jax.ShapeDtypeStruct((96, 256), BF)),
        in_specs=[vmem, hbm, pl.BlockSpec(memory_space=pltpu.SMEM), hbm, hbm, hbm],
        out_specs=(vmem, vmem),
        scratch_shapes=list(SCRATCH.values()),
        compiler_params=pltpu.CompilerParams(collective_id=0, has_side_effects=True, vmem_limit_bytes=56 * 2**20),
    )(
        y_root.T,
        root_inverse,
        block_map,
        y_child.reshape(16, 96, 256),
        panel.reshape(2, 768, 256),
        child_inverse.reshape(8, 2, 96, 768),
    )
    return x_root, x_child[None]


def solution(mesh):
    in_specs = (
        P("col", ("leaf", "row")),
        P(("leaf", "row"), "col"),
        P(),
        P("leaf", "row", None),
        P("leaf", "row", "col"),
        P("leaf", "row", "col"),
    )
    out_specs = (P(("leaf", "row", "col"), None), P("leaf", ("row", "col"), None))
    return jax.shard_map(per_device, mesh=mesh, in_specs=in_specs, out_specs=out_specs, check_vma=False)
```

```python
import jax
import jax.numpy as jnp
from jax import lax
from jax.experimental import pallas as pl
from jax.experimental.pallas import tpu as pltpu
from jax.sharding import PartitionSpec as P

MESH = pl.DeviceIdType.MESH
BF, F32 = jnp.bfloat16, jnp.float32

LEAF, ROW, COL, CHIP = 4, 8, 16, 8
NH = 2
W = 256 // NH

DMA = pltpu.SemaphoreType.DMA
SCRATCH = dict(
    inv_v=pltpu.VMEM((512, 1024), BF),
    panel_v=pltpu.VMEM((2, 768, 256), BF),
    cinv_v=pltpu.VMEM((2, 8, 96, 768), BF),
    yc_v=pltpu.VMEM((96, 256), BF),
    load=DMA((5,)),
    ya=pltpu.VMEM((LEAF, ROW, 16, 256), BF),
    yb=pltpu.VMEM((LEAF, ROW, 16, 256), BF),
    ya_s=DMA((LEAF, ROW)),
    ya_r=DMA((LEAF, ROW)),
    yb_s=DMA((LEAF, ROW)),
    yb_r=DMA((LEAF, ROW)),
    xpart=pltpu.VMEM((COL, 2, 16, 256), BF),
    xin=pltpu.VMEM((COL - 1, 2, 16, 256), BF),
    xin_s=DMA((COL - 1,)),
    xin_r=DMA((COL - 1,)),
    xpair=pltpu.VMEM((2, 2, 16, 256), BF),
    swap_s=DMA((1,)),
    swap_r=DMA((1,)),
    xg=pltpu.VMEM((16, 16, 256), BF),
    xg_s=DMA((ROW - 1,)),
    xg_r=DMA((ROW - 1,)),
    picked=pltpu.VMEM((COL - 1, 16, 256), BF),
    sel=pltpu.VMEM((COL, 16, 256), BF),
    sel_s=DMA((COL - 1,)),
    sel_r=DMA((COL - 1,)),
    xo=pltpu.VMEM((2, 16, 256), BF),
    xo_s=DMA((2,)),
    xo_r=DMA((2,)),
    pother=pltpu.VMEM((NH, 8, 96, W), BF),
    pin=pltpu.VMEM((NH, 8, 96, W), BF),
    pin_s=DMA((NH,)),
    pin_r=DMA((NH,)),
    pown=pltpu.VMEM((NH, 8, 96, W), F32),
    pout=pltpu.VMEM((NH, CHIP - 1, 96, W), BF),
    prx=pltpu.VMEM((NH, CHIP - 1, 96, W), BF),
    prx_s=DMA((NH, CHIP - 1)),
    prx_r=DMA((NH, CHIP - 1)),
    red=pltpu.VMEM((NH, 96, W), BF),
    rf=pltpu.VMEM((NH, CHIP, 96, W), BF),
    rf_s=DMA((NH, ROW)),
    rf_r=DMA((NH, CHIP)),
    cother=pltpu.VMEM((NH, 8, 96, W), BF),
    cin=pltpu.VMEM((NH, 8, 96, W), BF),
    cin_s=DMA((NH,)),
    cin_r=DMA((NH,)),
    cown=pltpu.VMEM((NH, 8, 96, W), F32),
    cout=pltpu.VMEM((NH, CHIP - 1, 96, W), BF),
    crx=pltpu.VMEM((NH, CHIP - 1, 96, W), BF),
    crx_s=DMA((NH, CHIP - 1)),
    crx_r=DMA((NH, CHIP - 1)),
)


class Refs:
    pass


def kernel(y_ref, inv_ref, map_ref, yc_ref, panel_ref, cinv_ref, xroot_ref, xchild_ref, *scratch):
    k = Refs()
    for name, ref in zip(SCRATCH, scratch):
        setattr(k, name, ref)
    leaf, row, col = lax.axis_index("leaf"), lax.axis_index("row"), lax.axis_index("col")
    core, chip = col % 2, col // 2
    sent = []

    def remote(src, dst, send, recv, device):
        return pltpu.make_async_remote_copy(
            src_ref=src, dst_ref=dst, send_sem=send, recv_sem=recv, device_id=device, device_id_type=MESH
        )

    def go(copy):
        copy.start()
        sent.append(copy)

    def leaf_peer(p):
        return ((leaf + p) % LEAF, row, col)

    def row_peer(p):
        return (leaf, (row + p) % ROW, col)

    def col_peer(p):
        return (leaf, row, (col + p) % COL)

    def chip_peer(p):
        return (leaf, row, 2 * ((chip + p) % CHIP) + core)

    twin = (leaf, row, col + 1 - 2 * core)

    def band_peer(p):
        return (leaf, (row + p) % ROW, 2 * row + core)


    loads = [
        pltpu.make_async_copy(inv_ref, k.inv_v, k.load.at[0]),
        pltpu.make_async_copy(panel_ref, k.panel_v, k.load.at[1]),
        pltpu.make_async_copy(yc_ref.at[8 * core + chip], k.yc_v, k.load.at[2]),
        pltpu.make_async_copy(cinv_ref.at[:, 0], k.cinv_v.at[0], k.load.at[3]),
        pltpu.make_async_copy(cinv_ref.at[:, 1], k.cinv_v.at[1], k.load.at[4]),
    ]
    for load in loads:
        load.start()

    barrier = pltpu.get_barrier_semaphore()

    def greet(device):
        pl.semaphore_signal(barrier, inc=1, device_id=device, device_id_type=MESH)

    for p in range(1, LEAF):
        greet(leaf_peer(p))
    for p in range(1, ROW):
        greet(row_peer(p))
    for p in range(1, COL):
        greet(col_peer(p))

    @pl.when(chip != row)
    def _():
        for p in range(1, CHIP):
            greet((leaf, chip, 2 * ((chip + p) % CHIP) + core))

    y = y_ref[...].astype(F32)
    for part, at in ((k.ya, 0), (k.yb, 512)):
        part[leaf, row] = jnp.concatenate([y[:, at : at + 256], y[:, at + 256 : at + 512]], axis=0).astype(BF)

    pl.semaphore_wait(barrier, LEAF - 1 + ROW - 1 + COL - 1 + jnp.where(chip == row, 0, CHIP - 1))

    def a_copy(a, p):
        if p == 0:
            part = k.ya.at[leaf, row]
            return remote(part, part, k.ya_s.at[a, 0], k.ya_r.at[a, 0], leaf_peer(a))
        part = k.ya.at[(leaf - a + LEAF) % LEAF, row]
        return remote(part, part, k.ya_s.at[a, p], k.ya_r.at[a, p], row_peer(p))

    def b_copy(a, p):
        if a == 0:
            part = k.yb.at[leaf, row]
            return remote(part, part, k.yb_s.at[0, p], k.yb_r.at[0, p], row_peer(p))
        part = k.yb.at[leaf, (row - p + ROW) % ROW]
        return remote(part, part, k.yb_s.at[a, p], k.yb_r.at[a, p], leaf_peer(a))

    leaf_order, row_order = (1, 3, 2), (1, 7, 2, 6, 3, 5, 4)
    for a in leaf_order:
        go(a_copy(a, 0))
    for p in row_order:
        go(b_copy(0, p))
    for a in leaf_order:
        go(b_copy(a, 0))
    for p in row_order:
        go(a_copy(0, p))
    near = [("b", 1), ("b", 7), ("a", 1), ("a", 3), ("b", 2), ("b", 6), ("b", 3), ("b", 5), ("a", 2), ("b", 4)]
    for which, n in near:
        if which == "a":
            a_copy(n, 0).wait_recv()
            for p in row_order:
                go(a_copy(n, p))
        else:
            b_copy(0, n).wait_recv()
            for a in leaf_order:
                go(b_copy(a, n))

    flight = {}

    def send_all(name, h, copies):
        for copy in copies:
            go(copy)
        flight[name, h] = copies

    def arrived(name, h):
        for copy in flight.pop((name, h)):
            copy.wait_recv()

    def root_mm():
        loads[0].wait()
        total = None
        for half, part in enumerate((k.ya, k.yb)):
            for a in range(LEAF):
                for p in range(ROW):
                    if half == 0 and p:
                        a_copy(a, p).wait_recv()
                    if half == 1 and a:
                        b_copy(a, p).wait_recv()
            y = part[...].astype(F32)
            for sub in range(2):
                at = 512 * half + 256 * sub
                term = lax.dot_general(
                    k.inv_v[:, at : at + 256],
                    y[:, :, 8 * sub : 8 * sub + 8, :].reshape(256, 256).astype(BF),
                    (((1,), (1,)), ((), ())),
                    preferred_element_type=F32,
                )
                total = term if total is None else total + term
        total = total.astype(BF)
        for block in range(2):
            k.xpart[:, block] = total[256 * block : 256 * block + 256].reshape(COL, 16, 256)
        send_all(
            "x",
            0,
            [
                remote(k.xpart.at[(col + p) % COL], k.xin.at[p - 1], k.xin_s.at[p - 1], k.xin_r.at[p - 1], col_peer(p))
                for p in range(1, COL)
            ],
        )

    def root_sum():
        arrived("x", 0)
        total = k.xpart[col].astype(F32)
        for p in range(COL - 1):
            total = total + k.xin[p].astype(F32)
        k.xpair[0] = total.astype(BF)
        send_all("swap", 0, [remote(k.xpair.at[0], k.xpair.at[1], k.swap_s.at[0], k.swap_r.at[0], leaf_peer(2))])
        root_out()

    def root_copy(block):
        target = 8 * block + col // 2
        return target, remote(
            k.xpair.at[0, block], k.xo.at[col % 2], k.xo_s.at[block], k.xo_r.at[col % 2], (leaf, row, target)
        )

    def root_out():
        for block in range(2):
            target, copy = root_copy(block)

            @pl.when(target != col)
            def _():
                copy.start()

            @pl.when(target == col)
            def _():
                k.xo[col % 2] = k.xpair[0, block]

    def root_finish():
        for block in range(2):
            target, copy = root_copy(block)

            @pl.when(target != col)
            def _():
                copy.wait_send()

        for slot in range(2):

            @pl.when(2 * (col % 8) + slot != col)
            def _():
                remote(k.xpair.at[0, 0], k.xo.at[slot], k.xo_s.at[0], k.xo_r.at[slot], (leaf, row, col)).wait_recv()

            xroot_ref[16 * slot : 16 * slot + 16, :] = k.xo[slot]

    def y_spread():
        arrived("swap", 0)
        swapped = jnp.where(map_ref[leaf, 0] // 16 == leaf, 0, 1)
        mine = k.xg.at[pl.ds(2 * row, 2)]
        k.xg[pl.ds(2 * row, 2)] = k.xpair[swapped]
        send_all(
            "g",
            0,
            [remote(mine, mine, k.xg_s.at[p - 1], k.xg_r.at[p - 1], row_peer(p)) for p in range(1, ROW)],
        )

    def col_spread():
        arrived("g", 0)
        copies = []
        for p in range(1, COL):
            k.picked[p - 1] = k.xg[map_ref[leaf, (col + p) % COL] % 16]
            copies.append(remote(k.picked.at[p - 1], k.sel.at[col], k.sel_s.at[p - 1], k.sel_r.at[p - 1], col_peer(p)))
            go(copies[-1])
        flight["sel", 0] = copies
        k.sel[col] = k.xg[map_ref[leaf, col] % 16]

    def times(tile, right):
        return jnp.dot(tile, right, preferred_element_type=F32).reshape(8, 96, W)

    def panel_mm(h):
        if h == 0:
            loads[1].wait()
            arrived("sel", 0)
        right = k.sel[:, :, h * W : (h + 1) * W].reshape(256, W)
        k.pother[h] = times(k.panel_v[1 - core], right).astype(BF)
        send_all("pin", h, [remote(k.pother.at[h], k.pin.at[h], k.pin_s.at[h], k.pin_r.at[h], twin)])
        k.pown[h] = times(k.panel_v[core], right)

    def scatter(h, name, own, inc, out, rx, send, recv):
        copies = []
        for p in range(1, CHIP):
            at = (chip + p) % CHIP
            out[h, p - 1] = (own[h, at] + inc[h, at].astype(F32)).astype(BF)
            copies.append(remote(out.at[h, p - 1], rx.at[h, p - 1], send.at[h, p - 1], recv.at[h, p - 1], chip_peer(p)))
            go(copies[-1])
        flight[name, h] = copies

    def gathered(h, own, inc, rx):
        total = own[h, chip] + inc[h, chip].astype(F32)
        for p in range(CHIP - 1):
            total = total + rx[h, p].astype(F32)
        return total

    def panel_rs(h):
        arrived("pin", h)
        scatter(h, "prx", k.pown, k.pin, k.pout, k.prx, k.prx_s, k.prx_r)

    def band_copy(h, p):
        return remote(k.red.at[h], k.rf.at[h, chip], k.rf_s.at[h, p], k.rf_r.at[h, chip], band_peer(p))

    def panel_sum(h):
        if h == 0:
            loads[2].wait()
        arrived("prx", h)
        yc = k.yc_v[:, h * W : (h + 1) * W].astype(F32)
        k.red[h] = (yc - gathered(h, k.pown, k.pin, k.prx)).astype(BF)
        for p in (4, 3, 5, 2, 6, 1, 7):
            go(band_copy(h, p))

        @pl.when(chip != row)
        def _():
            band_copy(h, 0).start()

        @pl.when(chip == row)
        def _():
            k.rf[h, chip] = k.red[h]

    def band_arrived(h):
        def wait(q):
            remote(k.red.at[h], k.rf.at[h, q], k.rf_s.at[h, 0], k.rf_r.at[h, q], band_peer(0)).wait_recv()

        for p in range(1, CHIP):
            wait((chip + p) % CHIP)

        @pl.when(chip != row)
        def _():
            wait(chip)
            band_copy(h, 0).wait_send()

    def child_mm(h):
        if h == 0:
            loads[3].wait()
            loads[4].wait()
        band_arrived(h)
        right = k.rf[h].reshape(768, W)
        k.cother[h] = times(k.cinv_v[1 - core].reshape(768, 768), right).astype(BF)
        send_all("cin", h, [remote(k.cother.at[h], k.cin.at[h], k.cin_s.at[h], k.cin_r.at[h], twin)])
        k.cown[h] = times(k.cinv_v[core].reshape(768, 768), right)

    def child_rs(h):
        arrived("cin", h)
        scatter(h, "crx", k.cown, k.cin, k.cout, k.crx, k.crx_s, k.crx_r)

    def child_sum(h):
        arrived("crx", h)
        xchild_ref[:, h * W : (h + 1) * W] = gathered(h, k.cown, k.cin, k.crx).astype(BF)

    root_mm()
    root_sum()
    y_spread()
    col_spread()
    stages = [panel_mm, panel_rs, panel_sum, child_mm, child_rs, child_sum]
    for t in range(len(stages) + NH - 1):
        for h in range(NH):
            if 0 <= t - h < len(stages):
                stages[t - h](h)
    root_finish()
    for copy in sent:
        copy.wait_send()


def per_device(y_root, root_inverse, block_map, y_child, panel, child_inverse):
    vmem = pl.BlockSpec(memory_space=pltpu.VMEM)
    hbm = pl.BlockSpec(memory_space=pl.ANY)
    x_root, x_child = pl.pallas_call(
        kernel,
        out_shape=(jax.ShapeDtypeStruct((32, 256), BF), jax.ShapeDtypeStruct((96, 256), BF)),
        in_specs=[vmem, hbm, pl.BlockSpec(memory_space=pltpu.SMEM), hbm, hbm, hbm],
        out_specs=(vmem, vmem),
        scratch_shapes=list(SCRATCH.values()),
        compiler_params=pltpu.CompilerParams(collective_id=0, has_side_effects=True, vmem_limit_bytes=56 * 2**20),
    )(
        y_root.T,
        root_inverse,
        block_map,
        y_child.reshape(16, 96, 256),
        panel.reshape(2, 768, 256),
        child_inverse.reshape(8, 2, 96, 768),
    )
    return x_root, x_child[None]


def solution(mesh):
    in_specs = (
        P("col", ("leaf", "row")),
        P(("leaf", "row"), "col"),
        P(),
        P("leaf", "row", None),
        P("leaf", "row", "col"),
        P("leaf", "row", "col"),
    )
    out_specs = (P(("leaf", "row", "col"), None), P("leaf", ("row", "col"), None))
    return jax.shard_map(per_device, mesh=mesh, in_specs=in_specs, out_specs=out_specs, check_vma=False)
```

```python
import jax
import jax.numpy as jnp
from jax import lax
from jax.experimental import pallas as pl
from jax.experimental.pallas import tpu as pltpu
from jax.sharding import PartitionSpec as P

MESH = pl.DeviceIdType.MESH
BF, F32 = jnp.bfloat16, jnp.float32

LEAF, ROW, COL, CHIP = 4, 8, 16, 8
NH = 2
W = 256 // NH

DMA = pltpu.SemaphoreType.DMA
SCRATCH = dict(
    inv_v=pltpu.VMEM((512, 1024), BF),
    panel_v=pltpu.VMEM((2, 768, 256), BF),
    cinv_v=pltpu.VMEM((2, 8, 96, 768), BF),
    yc_v=pltpu.VMEM((96, 256), BF),
    y_v=pltpu.VMEM((8, 1024), BF),
    map_v=pltpu.SMEM((4, 16), jnp.int32),
    load=DMA((7,)),
    ya=pltpu.VMEM((LEAF, ROW, 16, 256), BF),
    yb=pltpu.VMEM((LEAF, ROW, 16, 256), BF),
    ya_s=DMA((LEAF, ROW)),
    ya_r=DMA((LEAF, ROW)),
    yb_s=DMA((LEAF, ROW)),
    yb_r=DMA((LEAF, ROW)),
    xpart=pltpu.VMEM((COL, 2, 16, 256), BF),
    xin=pltpu.VMEM((COL - 1, 2, 16, 256), BF),
    xin_s=DMA((COL - 1,)),
    xin_r=DMA((COL - 1,)),
    xpair=pltpu.VMEM((2, 2, 16, 256), BF),
    swap_s=DMA((1,)),
    swap_r=DMA((1,)),
    xg=pltpu.VMEM((16, 16, 256), BF),
    xg_s=DMA((ROW - 1,)),
    xg_r=DMA((ROW - 1,)),
    picked=pltpu.VMEM((COL - 1, 16, 256), BF),
    sel=pltpu.VMEM((COL, 16, 256), BF),
    sel_s=DMA((COL - 1,)),
    sel_r=DMA((COL - 1,)),
    xo=pltpu.VMEM((2, 16, 256), BF),
    xo_s=DMA((2,)),
    xo_r=DMA((2,)),
    pother=pltpu.VMEM((NH, 8, 96, W), BF),
    pin=pltpu.VMEM((NH, 8, 96, W), BF),
    pin_s=DMA((NH,)),
    pin_r=DMA((NH,)),
    pown=pltpu.VMEM((NH, 8, 96, W), F32),
    pout=pltpu.VMEM((NH, CHIP - 1, 96, W), BF),
    prx=pltpu.VMEM((NH, CHIP - 1, 96, W), BF),
    prx_s=DMA((NH, CHIP - 1)),
    prx_r=DMA((NH, CHIP - 1)),
    red=pltpu.VMEM((NH, 96, W), BF),
    rf=pltpu.VMEM((NH, CHIP, 96, W), BF),
    rf_s=DMA((NH, ROW)),
    rf_r=DMA((NH, CHIP)),
    cother=pltpu.VMEM((NH, 8, 96, W), BF),
    cin=pltpu.VMEM((NH, 8, 96, W), BF),
    cin_s=DMA((NH,)),
    cin_r=DMA((NH,)),
    cown=pltpu.VMEM((NH, 8, 96, W), F32),
    cout=pltpu.VMEM((NH, CHIP - 1, 96, W), BF),
    crx=pltpu.VMEM((NH, CHIP - 1, 96, W), BF),
    crx_s=DMA((NH, CHIP - 1)),
    crx_r=DMA((NH, CHIP - 1)),
)


class Refs:
    pass


def kernel(y_ref, inv_ref, map_ref, yc_ref, panel_ref, cinv_ref, both_ref, *scratch):
    k = Refs()
    for name, ref in zip(SCRATCH, scratch):
        setattr(k, name, ref)
    leaf, row, col = lax.axis_index("leaf"), lax.axis_index("row"), lax.axis_index("col")
    core, chip = col % 2, col // 2
    sent = []

    def remote(src, dst, send, recv, device):
        return pltpu.make_async_remote_copy(
            src_ref=src, dst_ref=dst, send_sem=send, recv_sem=recv, device_id=device, device_id_type=MESH
        )

    def go(copy):
        copy.start()
        sent.append(copy)

    def drain(keep):
        while len(sent) > keep:
            sent.pop(0).wait_send()

    def leaf_peer(p):
        return ((leaf + p) % LEAF, row, col)

    def row_peer(p):
        return (leaf, (row + p) % ROW, col)

    def col_peer(p):
        return (leaf, row, (col + p) % COL)

    def chip_peer(p):
        return (leaf, row, 2 * ((chip + p) % CHIP) + core)

    twin = (leaf, row, col + 1 - 2 * core)

    def band_peer(p):
        return (leaf, (row + p) % ROW, 2 * row + core)


    loads = [
        pltpu.make_async_copy(inv_ref, k.inv_v, k.load.at[0]),
        pltpu.make_async_copy(panel_ref, k.panel_v, k.load.at[1]),
        pltpu.make_async_copy(yc_ref.at[8 * core + chip], k.yc_v, k.load.at[2]),
        pltpu.make_async_copy(cinv_ref.at[:, 0], k.cinv_v.at[0], k.load.at[3]),
        pltpu.make_async_copy(cinv_ref.at[:, 1], k.cinv_v.at[1], k.load.at[4]),
    ]
    small = [
        pltpu.make_async_copy(y_ref, k.y_v, k.load.at[5]),
        pltpu.make_async_copy(map_ref, k.map_v, k.load.at[6]),
    ]
    for load in small + loads:
        load.start()

    barrier = pltpu.get_barrier_semaphore()

    def greet(device):
        pl.semaphore_signal(barrier, inc=1, device_id=device, device_id_type=MESH)

    for p in range(1, LEAF):
        greet(leaf_peer(p))
    for p in range(1, ROW):
        greet(row_peer(p))
    for p in range(1, COL):
        greet(col_peer(p))

    @pl.when(chip != row)
    def _():
        for p in range(1, CHIP):
            greet((leaf, chip, 2 * ((chip + p) % CHIP) + core))

    small[0].wait()
    y = k.y_v[...].astype(F32)
    for part, at in ((k.ya, 0), (k.yb, 512)):
        part[leaf, row] = jnp.concatenate([y[:, at : at + 256], y[:, at + 256 : at + 512]], axis=0).astype(BF)

    pl.semaphore_wait(barrier, LEAF - 1 + ROW - 1 + COL - 1 + jnp.where(chip == row, 0, CHIP - 1))

    def a_copy(a, p):
        if p == 0:
            part = k.ya.at[leaf, row]
            return remote(part, part, k.ya_s.at[a, 0], k.ya_r.at[a, 0], leaf_peer(a))
        part = k.ya.at[(leaf - a + LEAF) % LEAF, row]
        return remote(part, part, k.ya_s.at[a, p], k.ya_r.at[a, p], row_peer(p))

    def b_copy(a, p):
        if a == 0:
            part = k.yb.at[leaf, row]
            return remote(part, part, k.yb_s.at[0, p], k.yb_r.at[0, p], row_peer(p))
        part = k.yb.at[leaf, (row - p + ROW) % ROW]
        return remote(part, part, k.yb_s.at[a, p], k.yb_r.at[a, p], leaf_peer(a))

    leaf_order, row_order = (1, 3, 2), (1, 7, 2, 6, 3, 5, 4)
    for a in leaf_order:
        go(a_copy(a, 0))
    for p in row_order:
        go(b_copy(0, p))
    for a in leaf_order:
        go(b_copy(a, 0))
    for p in row_order:
        go(a_copy(0, p))
    near = [("b", 1), ("b", 7), ("a", 1), ("a", 3), ("b", 2), ("b", 6), ("b", 3), ("b", 5), ("a", 2), ("b", 4)]
    for which, n in near:
        if which == "a":
            a_copy(n, 0).wait_recv()
            for p in row_order:
                go(a_copy(n, p))
        else:
            b_copy(0, n).wait_recv()
            for a in leaf_order:
                go(b_copy(a, n))

    flight = {}

    def send_all(name, h, copies):
        for copy in copies:
            go(copy)
        flight[name, h] = copies
        if name in ("swap", "g"):
            drain(len(copies) + COL)

    def arrived(name, h):
        for copy in flight.pop((name, h)):
            copy.wait_recv()

    def root_mm():
        loads[0].wait()
        total = None
        for half, part in enumerate((k.ya, k.yb)):
            for a in range(LEAF):
                for p in range(ROW):
                    if half == 0 and p:
                        a_copy(a, p).wait_recv()
                    if half == 1 and a:
                        b_copy(a, p).wait_recv()
            y = part[...].astype(F32)
            for sub in range(2):
                at = 512 * half + 256 * sub
                term = lax.dot_general(
                    k.inv_v[:, at : at + 256],
                    y[:, :, 8 * sub : 8 * sub + 8, :].reshape(256, 256).astype(BF),
                    (((1,), (1,)), ((), ())),
                    preferred_element_type=F32,
                )
                total = term if total is None else total + term
        total = total.astype(BF)
        for block in range(2):
            k.xpart[:, block] = total[256 * block : 256 * block + 256].reshape(COL, 16, 256)
        send_all(
            "x",
            0,
            [
                remote(k.xpart.at[(col + p) % COL], k.xin.at[p - 1], k.xin_s.at[p - 1], k.xin_r.at[p - 1], col_peer(p))
                for p in range(1, COL)
            ],
        )

    def root_sum():
        arrived("x", 0)
        total = k.xpart[col].astype(F32)
        for p in range(COL - 1):
            total = total + k.xin[p].astype(F32)
        k.xpair[0] = total.astype(BF)
        send_all("swap", 0, [remote(k.xpair.at[0], k.xpair.at[1], k.swap_s.at[0], k.swap_r.at[0], leaf_peer(2))])
        root_out()

    def root_copy(block):
        target = 8 * block + col // 2
        return target, remote(
            k.xpair.at[0, block], k.xo.at[col % 2], k.xo_s.at[block], k.xo_r.at[col % 2], (leaf, row, target)
        )

    def root_out():
        for block in range(2):
            target, copy = root_copy(block)

            @pl.when(target != col)
            def _():
                copy.start()

            @pl.when(target == col)
            def _():
                k.xo[col % 2] = k.xpair[0, block]

    def root_finish():
        for block in range(2):
            target, copy = root_copy(block)

            @pl.when(target != col)
            def _():
                copy.wait_send()

        for slot in range(2):

            @pl.when(2 * (col % 8) + slot != col)
            def _():
                remote(k.xpair.at[0, 0], k.xo.at[slot], k.xo_s.at[0], k.xo_r.at[slot], (leaf, row, col)).wait_recv()

            both_ref[16 * slot : 16 * slot + 16, :] = k.xo[slot]

    def y_spread():
        arrived("swap", 0)
        small[1].wait()
        swapped = jnp.where(k.map_v[leaf, 0] // 16 == leaf, 0, 1)
        mine = k.xg.at[pl.ds(2 * row, 2)]
        k.xg[pl.ds(2 * row, 2)] = k.xpair[swapped]
        send_all(
            "g",
            0,
            [remote(mine, mine, k.xg_s.at[p - 1], k.xg_r.at[p - 1], row_peer(p)) for p in range(1, ROW)],
        )

    def col_spread():
        arrived("g", 0)
        for p in range(1, COL):
            k.picked[p - 1] = k.xg[k.map_v[leaf, (col + p) % COL] % 16]
        copies = [
            remote(k.picked.at[p - 1], k.sel.at[col], k.sel_s.at[p - 1], k.sel_r.at[p - 1], col_peer(p)) for p in range(1, COL)
        ]
        for copy in copies:
            go(copy)
        flight["sel", 0] = copies
        k.sel[col] = k.xg[k.map_v[leaf, col] % 16]
        drain(COL - 1)

    def times(tile, right):
        return jnp.dot(tile, right, preferred_element_type=F32).reshape(8, 96, W)

    def panel_mm(h):
        if h == 0:
            loads[1].wait()
            arrived("sel", 0)
        right = k.sel[:, :, h * W : (h + 1) * W].reshape(256, W)
        k.pother[h] = times(k.panel_v[1 - core], right).astype(BF)
        send_all("pin", h, [remote(k.pother.at[h], k.pin.at[h], k.pin_s.at[h], k.pin_r.at[h], twin)])
        k.pown[h] = times(k.panel_v[core], right)

    def scatter(h, name, own, inc, out, rx, send, recv):
        copies = []
        for p in (2, 6, 1, 3, 5, 7, 4):
            at = (chip + p) % CHIP
            out[h, p - 1] = (own[h, at] + inc[h, at].astype(F32)).astype(BF)
            copies.append(remote(out.at[h, p - 1], rx.at[h, p - 1], send.at[h, p - 1], recv.at[h, p - 1], chip_peer(p)))
            go(copies[-1])
        flight[name, h] = copies
        drain(2 * CHIP)

    def gathered(h, own, inc, rx):
        total = own[h, chip] + inc[h, chip].astype(F32)
        for p in range(CHIP - 1):
            total = total + rx[h, p].astype(F32)
        return total

    def panel_rs(h):
        arrived("pin", h)
        scatter(h, "prx", k.pown, k.pin, k.pout, k.prx, k.prx_s, k.prx_r)

    def band_copy(h, p):
        return remote(k.red.at[h], k.rf.at[h, chip], k.rf_s.at[h, p], k.rf_r.at[h, chip], band_peer(p))

    def panel_sum(h):
        if h == 0:
            loads[2].wait()
        arrived("prx", h)
        yc = k.yc_v[:, h * W : (h + 1) * W].astype(F32)
        k.red[h] = (yc - gathered(h, k.pown, k.pin, k.prx)).astype(BF)
        for p in (4, 3, 5, 2, 6, 1, 7):
            go(band_copy(h, p))

        @pl.when(chip != row)
        def _():
            band_copy(h, 0).start()

        @pl.when(chip == row)
        def _():
            k.rf[h, chip] = k.red[h]

        drain(2 * CHIP)

    def band_arrived(h):
        def wait(q):
            remote(k.red.at[h], k.rf.at[h, q], k.rf_s.at[h, 0], k.rf_r.at[h, q], band_peer(0)).wait_recv()

        for p in range(1, CHIP):
            wait((chip + p) % CHIP)

        @pl.when(chip != row)
        def _():
            wait(chip)
            band_copy(h, 0).wait_send()

    def child_mm(h):
        if h == 0:
            loads[3].wait()
            loads[4].wait()
        band_arrived(h)
        right = k.rf[h].reshape(768, W)
        k.cother[h] = times(k.cinv_v[1 - core].reshape(768, 768), right).astype(BF)
        send_all("cin", h, [remote(k.cother.at[h], k.cin.at[h], k.cin_s.at[h], k.cin_r.at[h], twin)])
        k.cown[h] = times(k.cinv_v[core].reshape(768, 768), right)

    def child_rs(h):
        arrived("cin", h)
        scatter(h, "crx", k.cown, k.cin, k.cout, k.crx, k.crx_s, k.crx_r)

    def child_sum(h):
        arrived("crx", h)
        both_ref[32:, h * W : (h + 1) * W] = gathered(h, k.cown, k.cin, k.crx).astype(BF)

    root_mm()
    root_sum()
    y_spread()
    col_spread()
    stages = [panel_mm, panel_rs, panel_sum, child_mm, child_rs, child_sum]
    for stage in stages:
        for h in range(NH):
            stage(h)
    root_finish()
    for copy in sent:
        copy.wait_send()


def per_device(y_root, root_inverse, block_map, y_child, panel, child_inverse):
    vmem = pl.BlockSpec(memory_space=pltpu.VMEM)
    hbm = pl.BlockSpec(memory_space=pl.ANY)
    both = pl.pallas_call(
        kernel,
        out_shape=jax.ShapeDtypeStruct((128, 256), BF),
        in_specs=[hbm] * 6,
        out_specs=vmem,
        scratch_shapes=list(SCRATCH.values()),
        compiler_params=pltpu.CompilerParams(collective_id=0, has_side_effects=True, vmem_limit_bytes=56 * 2**20),
    )(
        y_root.T,
        root_inverse,
        block_map,
        y_child.reshape(16, 96, 256),
        panel.reshape(2, 768, 256),
        child_inverse.reshape(8, 2, 96, 768),
    )
    return both[:32], both[32:][None]


def solution(mesh):
    in_specs = (
        P("col", ("leaf", "row")),
        P(("leaf", "row"), "col"),
        P(),
        P("leaf", "row", None),
        P("leaf", "row", "col"),
        P("leaf", "row", "col"),
    )
    out_specs = (P(("leaf", "row", "col"), None), P("leaf", ("row", "col"), None))
    return jax.shard_map(per_device, mesh=mesh, in_specs=in_specs, out_specs=out_specs, check_vma=False)
```

```python
import jax
import jax.numpy as jnp
from jax import lax
from jax.experimental import pallas as pl
from jax.experimental.pallas import tpu as pltpu
from jax.sharding import PartitionSpec as P

MESH = pl.DeviceIdType.MESH
BF, F32 = jnp.bfloat16, jnp.float32

LEAF, ROW, COL, CHIP = 4, 8, 16, 8
NH = 2
W = 256 // NH

DMA = pltpu.SemaphoreType.DMA
SCRATCH = dict(
    inv_v=pltpu.VMEM((512, 1024), BF),
    panel_v=pltpu.VMEM((2, 768, 256), BF),
    cinv_v=pltpu.VMEM((2, 8, 96, 768), BF),
    yc_v=pltpu.VMEM((96, 256), BF),
    y_v=pltpu.VMEM((8, 1024), BF),
    map_v=pltpu.SMEM((4, 16), jnp.int32),
    load=DMA((7,)),
    ya=pltpu.VMEM((LEAF, ROW, 16, 256), BF),
    yb=pltpu.VMEM((LEAF, ROW, 16, 256), BF),
    ya_s=DMA((LEAF, ROW)),
    ya_r=DMA((LEAF, ROW)),
    yb_s=DMA((LEAF, ROW)),
    yb_r=DMA((LEAF, ROW)),
    xpart=pltpu.VMEM((NH, COL, 2, 16, W), BF),
    xin=pltpu.VMEM((NH, COL - 1, 2, 16, W), BF),
    xin_s=DMA((NH, COL - 1)),
    xin_r=DMA((NH, COL - 1)),
    **{f"xpair{h}": pltpu.VMEM((2, 2, 16, W), BF) for h in range(NH)},
    swap_s=DMA((NH,)),
    swap_r=DMA((NH,)),
    **{f"xg{h}": pltpu.VMEM((16, 16, W), BF) for h in range(NH)},
    xg_s=DMA((NH, ROW - 1)),
    xg_r=DMA((NH, ROW - 1)),
    picked=pltpu.VMEM((NH, COL - 1, 16, W), BF),
    sel=pltpu.VMEM((NH, COL, 16, W), BF),
    sel_s=DMA((NH, COL - 1)),
    sel_r=DMA((NH, COL - 1)),
    xo=pltpu.VMEM((2, NH, 16, W), BF),
    xo_s=DMA((NH, 2)),
    xo_r=DMA((NH, 2)),
    pother=pltpu.VMEM((NH, 8, 96, W), BF),
    pin=pltpu.VMEM((NH, 8, 96, W), BF),
    pin_s=DMA((NH,)),
    pin_r=DMA((NH,)),
    pown=pltpu.VMEM((NH, 8, 96, W), F32),
    pout=pltpu.VMEM((NH, CHIP - 1, 96, W), BF),
    prx=pltpu.VMEM((NH, CHIP - 1, 96, W), BF),
    prx_s=DMA((NH, CHIP - 1)),
    prx_r=DMA((NH, CHIP - 1)),
    red=pltpu.VMEM((NH, 96, W), BF),
    rf=pltpu.VMEM((NH, CHIP, 96, W), BF),
    rf_s=DMA((NH, ROW)),
    rf_r=DMA((NH, CHIP)),
    cother=pltpu.VMEM((NH, 8, 96, W), BF),
    cin=pltpu.VMEM((NH, 8, 96, W), BF),
    cin_s=DMA((NH,)),
    cin_r=DMA((NH,)),
    cown=pltpu.VMEM((NH, 8, 96, W), F32),
    cout=pltpu.VMEM((NH, CHIP - 1, 96, W), BF),
    crx=pltpu.VMEM((NH, CHIP - 1, 96, W), BF),
    crx_s=DMA((NH, CHIP - 1)),
    crx_r=DMA((NH, CHIP - 1)),
)


class Refs:
    pass


def kernel(y_ref, inv_ref, map_ref, yc_ref, panel_ref, cinv_ref, both_ref, *scratch):
    k = Refs()
    for name, ref in zip(SCRATCH, scratch):
        setattr(k, name, ref)
    xpair = [getattr(k, f"xpair{h}") for h in range(NH)]
    xg = [getattr(k, f"xg{h}") for h in range(NH)]
    leaf, row, col = lax.axis_index("leaf"), lax.axis_index("row"), lax.axis_index("col")
    core, chip = col % 2, col // 2
    sent = []

    def remote(src, dst, send, recv, device):
        return pltpu.make_async_remote_copy(
            src_ref=src, dst_ref=dst, send_sem=send, recv_sem=recv, device_id=device, device_id_type=MESH
        )

    def go(copy):
        copy.start()
        sent.append(copy)

    def drain(keep):
        while len(sent) > keep:
            sent.pop(0).wait_send()

    def leaf_peer(p):
        return ((leaf + p) % LEAF, row, col)

    def row_peer(p):
        return (leaf, (row + p) % ROW, col)

    def col_peer(p):
        return (leaf, row, (col + p) % COL)

    def chip_peer(p):
        return (leaf, row, 2 * ((chip + p) % CHIP) + core)

    twin = (leaf, row, col + 1 - 2 * core)

    def band_peer(p):
        return (leaf, (row + p) % ROW, 2 * row + core)


    loads = [
        pltpu.make_async_copy(inv_ref, k.inv_v, k.load.at[0]),
        pltpu.make_async_copy(panel_ref, k.panel_v, k.load.at[1]),
        pltpu.make_async_copy(yc_ref.at[8 * core + chip], k.yc_v, k.load.at[2]),
        pltpu.make_async_copy(cinv_ref.at[:, 0], k.cinv_v.at[0], k.load.at[3]),
        pltpu.make_async_copy(cinv_ref.at[:, 1], k.cinv_v.at[1], k.load.at[4]),
    ]
    small = [
        pltpu.make_async_copy(y_ref, k.y_v, k.load.at[5]),
        pltpu.make_async_copy(map_ref, k.map_v, k.load.at[6]),
    ]
    for load in small + loads:
        load.start()

    barrier = pltpu.get_barrier_semaphore()

    def greet(device):
        pl.semaphore_signal(barrier, inc=1, device_id=device, device_id_type=MESH)

    for p in range(1, LEAF):
        greet(leaf_peer(p))
    for p in range(1, ROW):
        greet(row_peer(p))
    for p in range(1, COL):
        greet(col_peer(p))

    @pl.when(chip != row)
    def _():
        for p in range(1, CHIP):
            greet((leaf, chip, 2 * ((chip + p) % CHIP) + core))

    small[0].wait()
    y = k.y_v[...].astype(F32)
    for part, at in ((k.ya, 0), (k.yb, 512)):
        part[leaf, row] = jnp.concatenate([y[:, at : at + 256], y[:, at + 256 : at + 512]], axis=0).astype(BF)

    pl.semaphore_wait(barrier, LEAF - 1 + ROW - 1 + COL - 1 + jnp.where(chip == row, 0, CHIP - 1))

    def a_copy(a, p):
        if p == 0:
            part = k.ya.at[leaf, row]
            return remote(part, part, k.ya_s.at[a, 0], k.ya_r.at[a, 0], leaf_peer(a))
        part = k.ya.at[(leaf - a + LEAF) % LEAF, row]
        return remote(part, part, k.ya_s.at[a, p], k.ya_r.at[a, p], row_peer(p))

    def b_copy(a, p):
        if a == 0:
            part = k.yb.at[leaf, row]
            return remote(part, part, k.yb_s.at[0, p], k.yb_r.at[0, p], row_peer(p))
        part = k.yb.at[leaf, (row - p + ROW) % ROW]
        return remote(part, part, k.yb_s.at[a, p], k.yb_r.at[a, p], leaf_peer(a))

    leaf_order, row_order = (1, 3, 2), (1, 7, 2, 6, 3, 5, 4)
    for a in leaf_order:
        go(a_copy(a, 0))
    for p in row_order:
        go(b_copy(0, p))
    for a in leaf_order:
        go(b_copy(a, 0))
    for p in row_order:
        go(a_copy(0, p))
    near = [("b", 1), ("b", 7), ("a", 1), ("a", 3), ("b", 2), ("b", 6), ("b", 3), ("b", 5), ("a", 2), ("b", 4)]
    for which, n in near:
        if which == "a":
            a_copy(n, 0).wait_recv()
            for p in row_order:
                go(a_copy(n, p))
        else:
            b_copy(0, n).wait_recv()
            for a in leaf_order:
                go(b_copy(a, n))

    flight = {}

    def send_all(name, h, copies):
        for copy in copies:
            go(copy)
        flight[name, h] = copies
        if name in ("swap", "g"):
            drain(len(copies) + COL)

    def arrived(name, h):
        for copy in flight.pop((name, h)):
            copy.wait_recv()

    def root_mm():
        loads[0].wait()
        total = None
        for half, part in enumerate((k.ya, k.yb)):
            for a in range(LEAF):
                for p in range(ROW):
                    if half == 0 and p:
                        a_copy(a, p).wait_recv()
                    if half == 1 and a:
                        b_copy(a, p).wait_recv()
            y = part[...].astype(F32)
            for sub in range(2):
                at = 512 * half + 256 * sub
                term = lax.dot_general(
                    k.inv_v[:, at : at + 256],
                    y[:, :, 8 * sub : 8 * sub + 8, :].reshape(256, 256).astype(BF),
                    (((1,), (1,)), ((), ())),
                    preferred_element_type=F32,
                )
                total = term if total is None else total + term
        total = total.astype(BF)
        for h in range(NH):
            for block in range(2):
                k.xpart[h, :, block] = total[256 * block : 256 * block + 256, h * W : (h + 1) * W].reshape(COL, 16, W)
            send_all(
                "x",
                h,
                [
                    remote(
                        k.xpart.at[h, (col + p) % COL], k.xin.at[h, p - 1], k.xin_s.at[h, p - 1], k.xin_r.at[h, p - 1], col_peer(p)
                    )
                    for p in range(1, COL)
                ],
            )

    def root_sum(h):
        arrived("x", h)
        total = k.xpart[h, col].astype(F32)
        for p in range(COL - 1):
            total = total + k.xin[h, p].astype(F32)
        xpair[h][0] = total.astype(BF)
        send_all("swap", h, [remote(xpair[h].at[0], xpair[h].at[1], k.swap_s.at[h], k.swap_r.at[h], leaf_peer(2))])
        root_out(h)

    def root_copy(h, block):
        target = 8 * block + col // 2
        return target, remote(
            xpair[h].at[0, block], k.xo.at[col % 2, h], k.xo_s.at[h, block], k.xo_r.at[h, col % 2], (leaf, row, target)
        )

    def root_out(h):
        for block in range(2):
            target, copy = root_copy(h, block)

            @pl.when(target != col)
            def _():
                copy.start()

            @pl.when(target == col)
            def _():
                k.xo[col % 2, h] = xpair[h][0, block]

    def root_finish(h):
        for block in range(2):
            target, copy = root_copy(h, block)

            @pl.when(target != col)
            def _():
                copy.wait_send()

        for slot in range(2):

            @pl.when(2 * (col % 8) + slot != col)
            def _():
                remote(xpair[h].at[0, 0], k.xo.at[slot, h], k.xo_s.at[h, 0], k.xo_r.at[h, slot], (leaf, row, col)).wait_recv()

            both_ref[16 * slot : 16 * slot + 16, h * W : (h + 1) * W] = k.xo[slot, h]

    def y_spread(h):
        arrived("swap", h)
        if h == 0:
            small[1].wait()
        swapped = jnp.where(k.map_v[leaf, 0] // 16 == leaf, 0, 1)
        mine = xg[h].at[pl.ds(2 * row, 2)]
        xg[h][pl.ds(2 * row, 2)] = xpair[h][swapped]
        send_all(
            "g",
            h,
            [remote(mine, mine, k.xg_s.at[h, p - 1], k.xg_r.at[h, p - 1], row_peer(p)) for p in (4, 3, 5, 2, 6, 1, 7)],
        )

    def col_spread(h):
        arrived("g", h)
        for p in range(1, COL):
            k.picked[h, p - 1] = xg[h][k.map_v[leaf, (col + p) % COL] % 16]
        copies = [
            remote(k.picked.at[h, p - 1], k.sel.at[h, col], k.sel_s.at[h, p - 1], k.sel_r.at[h, p - 1], col_peer(p))
            for p in range(1, COL)
        ]
        send_all("sel", h, copies)
        k.sel[h, col] = xg[h][k.map_v[leaf, col] % 16]

    def times(tile, right):
        return jnp.dot(tile, right, preferred_element_type=F32).reshape(8, 96, W)

    def panel_mm(h):
        if h == 0:
            loads[1].wait()
        arrived("sel", h)
        right = k.sel[h].reshape(256, W)
        k.pother[h] = times(k.panel_v[1 - core], right).astype(BF)
        send_all("pin", h, [remote(k.pother.at[h], k.pin.at[h], k.pin_s.at[h], k.pin_r.at[h], twin)])
        k.pown[h] = times(k.panel_v[core], right)

    def scatter(h, name, own, inc, out, rx, send, recv):
        copies = []
        for p in (2, 6, 1, 3, 5, 7, 4):
            at = (chip + p) % CHIP
            out[h, p - 1] = (own[h, at] + inc[h, at].astype(F32)).astype(BF)
            copies.append(remote(out.at[h, p - 1], rx.at[h, p - 1], send.at[h, p - 1], recv.at[h, p - 1], chip_peer(p)))
            go(copies[-1])
        flight[name, h] = copies
        drain(2 * CHIP)

    def gathered(h, own, inc, rx):
        total = own[h, chip] + inc[h, chip].astype(F32)
        for p in range(CHIP - 1):
            total = total + rx[h, p].astype(F32)
        return total

    def panel_rs(h):
        arrived("pin", h)
        scatter(h, "prx", k.pown, k.pin, k.pout, k.prx, k.prx_s, k.prx_r)

    def band_copy(h, p):
        return remote(k.red.at[h], k.rf.at[h, chip], k.rf_s.at[h, p], k.rf_r.at[h, chip], band_peer(p))

    def panel_sum(h):
        if h == 0:
            loads[2].wait()
        arrived("prx", h)
        yc = k.yc_v[:, h * W : (h + 1) * W].astype(F32)
        k.red[h] = (yc - gathered(h, k.pown, k.pin, k.prx)).astype(BF)
        for p in (4, 3, 5, 2, 6, 1, 7):
            go(band_copy(h, p))

        @pl.when(chip != row)
        def _():
            band_copy(h, 0).start()

        @pl.when(chip == row)
        def _():
            k.rf[h, chip] = k.red[h]

        drain(2 * CHIP)

    def band_arrived(h):
        def wait(q):
            remote(k.red.at[h], k.rf.at[h, q], k.rf_s.at[h, 0], k.rf_r.at[h, q], band_peer(0)).wait_recv()

        for p in range(1, CHIP):
            wait((chip + p) % CHIP)

        @pl.when(chip != row)
        def _():
            wait(chip)
            band_copy(h, 0).wait_send()

    def child_mm(h):
        if h == 0:
            loads[3].wait()
            loads[4].wait()
        band_arrived(h)
        right = k.rf[h].reshape(768, W)
        k.cother[h] = times(k.cinv_v[1 - core].reshape(768, 768), right).astype(BF)
        send_all("cin", h, [remote(k.cother.at[h], k.cin.at[h], k.cin_s.at[h], k.cin_r.at[h], twin)])
        k.cown[h] = times(k.cinv_v[core].reshape(768, 768), right)

    def child_rs(h):
        arrived("cin", h)
        scatter(h, "crx", k.cown, k.cin, k.cout, k.crx, k.crx_s, k.crx_r)

    def child_sum(h):
        arrived("crx", h)
        both_ref[32:, h * W : (h + 1) * W] = gathered(h, k.cown, k.cin, k.crx).astype(BF)

    root_mm()
    stages = [root_sum, y_spread, col_spread, panel_mm, panel_rs, panel_sum, child_mm, child_rs, child_sum]
    for stage in stages:
        for h in range(NH):
            stage(h)
            if stage is panel_sum:
                root_finish(h)
    for copy in sent:
        copy.wait_send()


def per_device(y_root, root_inverse, block_map, y_child, panel, child_inverse):
    vmem = pl.BlockSpec(memory_space=pltpu.VMEM)
    hbm = pl.BlockSpec(memory_space=pl.ANY)
    both = pl.pallas_call(
        kernel,
        out_shape=jax.ShapeDtypeStruct((128, 256), BF),
        in_specs=[hbm] * 6,
        out_specs=vmem,
        scratch_shapes=list(SCRATCH.values()),
        compiler_params=pltpu.CompilerParams(collective_id=0, has_side_effects=True, vmem_limit_bytes=56 * 2**20),
    )(
        y_root.T,
        root_inverse,
        block_map,
        y_child.reshape(16, 96, 256),
        panel.reshape(2, 768, 256),
        child_inverse.reshape(8, 2, 96, 768),
    )
    def split(both_ref, root_ref, child_ref):
        root_ref[...] = both_ref[:32]
        child_ref[0] = both_ref[32:]

    return pl.pallas_call(
        split,
        out_shape=(jax.ShapeDtypeStruct((32, 256), BF), jax.ShapeDtypeStruct((1, 96, 256), BF)),
        in_specs=[vmem],
        out_specs=(vmem, vmem),
    )(both)


def solution(mesh):
    in_specs = (
        P("col", ("leaf", "row")),
        P(("leaf", "row"), "col"),
        P(),
        P("leaf", "row", None),
        P("leaf", "row", "col"),
        P("leaf", "row", "col"),
    )
    out_specs = (P(("leaf", "row", "col"), None), P("leaf", ("row", "col"), None))
    return jax.shard_map(per_device, mesh=mesh, in_specs=in_specs, out_specs=out_specs, check_vma=False)
```

```python
import jax
import jax.numpy as jnp
from jax import lax
from jax.experimental import pallas as pl
from jax.experimental.pallas import tpu as pltpu
from jax.sharding import PartitionSpec as P

MESH = pl.DeviceIdType.MESH
BF, F32 = jnp.bfloat16, jnp.float32

LEAF, ROW, COL, CHIP = 4, 8, 16, 8
NH = 2
W = 256 // NH

DMA = pltpu.SemaphoreType.DMA
SCRATCH = dict(
    inv_v=pltpu.VMEM((512, 1024), BF),
    panel_v=pltpu.VMEM((2, 768, 256), BF),
    cinv_v=pltpu.VMEM((2, 8, 96, 768), BF),
    yc_v=pltpu.VMEM((96, 256), BF),
    y_v=pltpu.VMEM((8, 1024), BF),
    map_v=pltpu.SMEM((4, 16), jnp.int32),
    load=DMA((7,)),
    ya=pltpu.VMEM((LEAF, ROW, 16, 256), BF),
    yb=pltpu.VMEM((LEAF, ROW, 16, 256), BF),
    ya_s=DMA((LEAF, ROW)),
    ya_r=DMA((LEAF, ROW)),
    yb_s=DMA((LEAF, ROW)),
    yb_r=DMA((LEAF, ROW)),
    xpart=pltpu.VMEM((NH, COL, 2, 16, W), BF),
    xin=pltpu.VMEM((NH, COL - 1, 2, 16, W), BF),
    xin_s=DMA((NH, COL - 1)),
    xin_r=DMA((NH, COL - 1)),
    **{f"xpair{h}": pltpu.VMEM((2, 2, 16, W), BF) for h in range(NH)},
    swap_s=DMA((NH,)),
    swap_r=DMA((NH,)),
    **{f"xg{h}": pltpu.VMEM((16, 16, W), BF) for h in range(NH)},
    xg_s=DMA((NH, ROW - 1)),
    xg_r=DMA((NH, ROW - 1)),
    picked=pltpu.VMEM((NH, COL - 1, 16, W), BF),
    sel=pltpu.VMEM((NH, COL, 16, W), BF),
    sel_s=DMA((NH, COL - 1)),
    sel_r=DMA((NH, COL - 1)),
    xo=pltpu.VMEM((2, NH, 16, W), BF),
    xo_s=DMA((NH, 2)),
    xo_r=DMA((NH, 2)),
    pother=pltpu.VMEM((NH, 8, 96, W), BF),
    pin=pltpu.VMEM((NH, 8, 96, W), BF),
    pin_s=DMA((NH,)),
    pin_r=DMA((NH,)),
    pown=pltpu.VMEM((NH, 8, 96, W), F32),
    pout=pltpu.VMEM((NH, CHIP - 1, 96, W), BF),
    prx=pltpu.VMEM((NH, CHIP - 1, 96, W), BF),
    prx_s=DMA((NH, CHIP - 1)),
    prx_r=DMA((NH, CHIP - 1)),
    red=pltpu.VMEM((NH, 96, W), BF),
    rf=pltpu.VMEM((NH, CHIP, 96, W), BF),
    rf_s=DMA((NH, ROW)),
    rf_r=DMA((NH, CHIP)),
    cother=pltpu.VMEM((NH, 8, 96, W), BF),
    cin=pltpu.VMEM((NH, 8, 96, W), BF),
    cin_s=DMA((NH,)),
    cin_r=DMA((NH,)),
    cown=pltpu.VMEM((NH, 8, 96, W), F32),
    cout=pltpu.VMEM((NH, CHIP - 1, 96, W), BF),
    crx=pltpu.VMEM((NH, CHIP - 1, 96, W), BF),
    crx_s=DMA((NH, CHIP - 1)),
    crx_r=DMA((NH, CHIP - 1)),
)


class Refs:
    pass


def kernel(y_ref, inv_ref, map_ref, yc_ref, panel_ref, cinv_ref, both_ref, *scratch):
    k = Refs()
    for name, ref in zip(SCRATCH, scratch):
        setattr(k, name, ref)
    xpair = [getattr(k, f"xpair{h}") for h in range(NH)]
    xg = [getattr(k, f"xg{h}") for h in range(NH)]
    leaf, row, col = lax.axis_index("leaf"), lax.axis_index("row"), lax.axis_index("col")
    core, chip = col % 2, col // 2
    sent = []

    def remote(src, dst, send, recv, device):
        return pltpu.make_async_remote_copy(
            src_ref=src, dst_ref=dst, send_sem=send, recv_sem=recv, device_id=device, device_id_type=MESH
        )

    def go(copy):
        copy.start()
        sent.append(copy)

    def drain(keep):
        while len(sent) > keep:
            sent.pop(0).wait_send()

    def leaf_peer(p):
        return ((leaf + p) % LEAF, row, col)

    def row_peer(p):
        return (leaf, (row + p) % ROW, col)

    def col_peer(p):
        return (leaf, row, (col + p) % COL)

    def chip_peer(p):
        return (leaf, row, 2 * ((chip + p) % CHIP) + core)

    twin = (leaf, row, col + 1 - 2 * core)

    def band_peer(p):
        return (leaf, (row + p) % ROW, 2 * row + core)


    loads = [
        pltpu.make_async_copy(inv_ref, k.inv_v, k.load.at[0]),
        pltpu.make_async_copy(panel_ref, k.panel_v, k.load.at[1]),
        pltpu.make_async_copy(yc_ref.at[8 * core + chip], k.yc_v, k.load.at[2]),
        pltpu.make_async_copy(cinv_ref.at[:, 0], k.cinv_v.at[0], k.load.at[3]),
        pltpu.make_async_copy(cinv_ref.at[:, 1], k.cinv_v.at[1], k.load.at[4]),
    ]
    small = [
        pltpu.make_async_copy(y_ref, k.y_v, k.load.at[5]),
        pltpu.make_async_copy(map_ref, k.map_v, k.load.at[6]),
    ]
    for load in small:
        load.start()

    barrier = pltpu.get_barrier_semaphore()

    def greet(device):
        pl.semaphore_signal(barrier, inc=1, device_id=device, device_id_type=MESH)

    for p in range(1, LEAF):
        greet(leaf_peer(p))
    for p in range(1, ROW):
        greet(row_peer(p))
    for p in range(1, COL):
        greet(col_peer(p))

    @pl.when(chip != row)
    def _():
        for p in range(1, CHIP):
            greet((leaf, chip, 2 * ((chip + p) % CHIP) + core))

    for load in loads:
        load.start()
    small[0].wait()
    y = k.y_v[...].astype(F32)
    for part, at in ((k.ya, 0), (k.yb, 512)):
        part[leaf, row] = jnp.concatenate([y[:, at : at + 256], y[:, at + 256 : at + 512]], axis=0).astype(BF)

    pl.semaphore_wait(barrier, LEAF - 1 + ROW - 1 + COL - 1 + jnp.where(chip == row, 0, CHIP - 1))

    def a_copy(a, p):
        if p == 0:
            part = k.ya.at[leaf, row]
            return remote(part, part, k.ya_s.at[a, 0], k.ya_r.at[a, 0], leaf_peer(a))
        part = k.ya.at[(leaf - a + LEAF) % LEAF, row]
        return remote(part, part, k.ya_s.at[a, p], k.ya_r.at[a, p], row_peer(p))

    def b_copy(a, p):
        if a == 0:
            part = k.yb.at[leaf, row]
            return remote(part, part, k.yb_s.at[0, p], k.yb_r.at[0, p], row_peer(p))
        part = k.yb.at[leaf, (row - p + ROW) % ROW]
        return remote(part, part, k.yb_s.at[a, p], k.yb_r.at[a, p], leaf_peer(a))

    leaf_order, row_order = (1, 3, 2), (1, 7, 2, 6, 3, 5, 4)
    for a in leaf_order:
        go(a_copy(a, 0))
    for p in row_order:
        go(b_copy(0, p))
    for a in leaf_order:
        go(b_copy(a, 0))
    for p in row_order:
        go(a_copy(0, p))
    near = [("b", 1), ("b", 7), ("a", 1), ("a", 3), ("b", 2), ("b", 6), ("b", 3), ("b", 5), ("a", 2), ("b", 4)]
    for which, n in near:
        if which == "a":
            a_copy(n, 0).wait_recv()
            for p in row_order:
                go(a_copy(n, p))
        else:
            b_copy(0, n).wait_recv()
            for a in leaf_order:
                go(b_copy(a, n))

    flight = {}

    def send_all(name, h, copies):
        for copy in copies:
            go(copy)
        flight[name, h] = copies
        if name in ("swap", "g"):
            drain(len(copies) + COL)

    def arrived(name, h):
        for copy in flight.pop((name, h)):
            copy.wait_recv()

    def root_mm():
        loads[0].wait()
        total = None
        for half, part in enumerate((k.ya, k.yb)):
            for a in range(LEAF):
                for p in range(ROW):
                    if half == 0 and p:
                        a_copy(a, p).wait_recv()
                    if half == 1 and a:
                        b_copy(a, p).wait_recv()
            y = part[...].astype(F32)
            for sub in range(2):
                at = 512 * half + 256 * sub
                term = lax.dot_general(
                    k.inv_v[:, at : at + 256],
                    y[:, :, 8 * sub : 8 * sub + 8, :].reshape(256, 256).astype(BF),
                    (((1,), (1,)), ((), ())),
                    preferred_element_type=F32,
                )
                total = term if total is None else total + term
        total = total.astype(BF)
        for h in range(NH):
            for block in range(2):
                k.xpart[h, :, block] = total[256 * block : 256 * block + 256, h * W : (h + 1) * W].reshape(COL, 16, W)
            send_all(
                "x",
                h,
                [
                    remote(
                        k.xpart.at[h, (col + p) % COL], k.xin.at[h, p - 1], k.xin_s.at[h, p - 1], k.xin_r.at[h, p - 1], col_peer(p)
                    )
                    for p in range(1, COL)
                ],
            )

    def root_sum(h):
        arrived("x", h)
        total = k.xpart[h, col].astype(F32)
        for p in range(COL - 1):
            total = total + k.xin[h, p].astype(F32)
        xpair[h][0] = total.astype(BF)
        send_all("swap", h, [remote(xpair[h].at[0], xpair[h].at[1], k.swap_s.at[h], k.swap_r.at[h], leaf_peer(2))])
        root_out(h)

    def root_copy(h, block):
        target = 8 * block + col // 2
        return target, remote(
            xpair[h].at[0, block], k.xo.at[col % 2, h], k.xo_s.at[h, block], k.xo_r.at[h, col % 2], (leaf, row, target)
        )

    def root_out(h):
        for block in range(2):
            target, copy = root_copy(h, block)

            @pl.when(target != col)
            def _():
                copy.start()

            @pl.when(target == col)
            def _():
                k.xo[col % 2, h] = xpair[h][0, block]

    def root_finish(h):
        for block in range(2):
            target, copy = root_copy(h, block)

            @pl.when(target != col)
            def _():
                copy.wait_send()

        for slot in range(2):

            @pl.when(2 * (col % 8) + slot != col)
            def _():
                remote(xpair[h].at[0, 0], k.xo.at[slot, h], k.xo_s.at[h, 0], k.xo_r.at[h, slot], (leaf, row, col)).wait_recv()

            both_ref[16 * slot : 16 * slot + 16, h * W : (h + 1) * W] = k.xo[slot, h]

    def y_spread(h):
        arrived("swap", h)
        if h == 0:
            small[1].wait()
        swapped = jnp.where(k.map_v[leaf, 0] // 16 == leaf, 0, 1)
        mine = xg[h].at[pl.ds(2 * row, 2)]
        xg[h][pl.ds(2 * row, 2)] = xpair[h][swapped]
        send_all(
            "g",
            h,
            [remote(mine, mine, k.xg_s.at[h, p - 1], k.xg_r.at[h, p - 1], row_peer(p)) for p in (4, 3, 5, 2, 6, 1, 7)],
        )

    def col_spread(h):
        arrived("g", h)
        for p in range(1, COL):
            k.picked[h, p - 1] = xg[h][k.map_v[leaf, (col + p) % COL] % 16]
        copies = [
            remote(k.picked.at[h, p - 1], k.sel.at[h, col], k.sel_s.at[h, p - 1], k.sel_r.at[h, p - 1], col_peer(p))
            for p in range(1, COL)
        ]
        send_all("sel", h, copies)
        k.sel[h, col] = xg[h][k.map_v[leaf, col] % 16]

    def times(tile, right):
        return jnp.dot(tile, right, preferred_element_type=F32).reshape(8, 96, W)

    def panel_mm(h):
        if h == 0:
            loads[1].wait()
        arrived("sel", h)
        right = k.sel[h].reshape(256, W)
        k.pother[h] = times(k.panel_v[1 - core], right).astype(BF)
        send_all("pin", h, [remote(k.pother.at[h], k.pin.at[h], k.pin_s.at[h], k.pin_r.at[h], twin)])
        k.pown[h] = times(k.panel_v[core], right)

    def scatter(h, name, own, inc, out, rx, send, recv):
        copies = []
        for p in (2, 6, 1, 3, 5, 7, 4):
            at = (chip + p) % CHIP
            out[h, p - 1] = (own[h, at] + inc[h, at].astype(F32)).astype(BF)
            copies.append(remote(out.at[h, p - 1], rx.at[h, p - 1], send.at[h, p - 1], recv.at[h, p - 1], chip_peer(p)))
            go(copies[-1])
        flight[name, h] = copies
        drain(2 * CHIP)

    def gathered(h, own, inc, rx):
        total = own[h, chip] + inc[h, chip].astype(F32)
        for p in range(CHIP - 1):
            total = total + rx[h, p].astype(F32)
        return total

    def panel_rs(h):
        arrived("pin", h)
        scatter(h, "prx", k.pown, k.pin, k.pout, k.prx, k.prx_s, k.prx_r)

    def band_copy(h, p):
        return remote(k.red.at[h], k.rf.at[h, chip], k.rf_s.at[h, p], k.rf_r.at[h, chip], band_peer(p))

    def panel_sum(h):
        if h == 0:
            loads[2].wait()
        arrived("prx", h)
        yc = k.yc_v[:, h * W : (h + 1) * W].astype(F32)
        k.red[h] = (yc - gathered(h, k.pown, k.pin, k.prx)).astype(BF)
        for p in (4, 3, 5, 2, 6, 1, 7):
            go(band_copy(h, p))

        @pl.when(chip != row)
        def _():
            band_copy(h, 0).start()

        @pl.when(chip == row)
        def _():
            k.rf[h, chip] = k.red[h]

        drain(2 * CHIP)

    def band_arrived(h):
        def wait(q):
            remote(k.red.at[h], k.rf.at[h, q], k.rf_s.at[h, 0], k.rf_r.at[h, q], band_peer(0)).wait_recv()

        for p in range(1, CHIP):
            wait((chip + p) % CHIP)

        @pl.when(chip != row)
        def _():
            wait(chip)
            band_copy(h, 0).wait_send()

    def child_mm(h):
        if h == 0:
            loads[3].wait()
            loads[4].wait()
        band_arrived(h)
        right = k.rf[h].reshape(768, W)
        k.cother[h] = times(k.cinv_v[1 - core].reshape(768, 768), right).astype(BF)
        send_all("cin", h, [remote(k.cother.at[h], k.cin.at[h], k.cin_s.at[h], k.cin_r.at[h], twin)])
        k.cown[h] = times(k.cinv_v[core].reshape(768, 768), right)

    def child_rs(h):
        arrived("cin", h)
        scatter(h, "crx", k.cown, k.cin, k.cout, k.crx, k.crx_s, k.crx_r)

    def child_sum(h):
        arrived("crx", h)
        both_ref[32:, h * W : (h + 1) * W] = gathered(h, k.cown, k.cin, k.crx).astype(BF)

    root_mm()
    groups = [(root_sum,), (y_spread,), (col_spread,), (panel_mm,), (panel_rs,), (panel_sum,), (child_mm, child_rs), (child_sum,)]
    for group in groups:
        for h in range(NH):
            for stage in group:
                stage(h)
        if panel_sum in group:
            for h in range(NH):
                root_finish(h)
    for copy in sent:
        copy.wait_send()


def per_device(y_root, root_inverse, block_map, y_child, panel, child_inverse):
    vmem = pl.BlockSpec(memory_space=pltpu.VMEM)
    hbm = pl.BlockSpec(memory_space=pl.ANY)
    both = pl.pallas_call(
        kernel,
        out_shape=jax.ShapeDtypeStruct((128, 256), BF),
        in_specs=[hbm] * 6,
        out_specs=vmem,
        scratch_shapes=list(SCRATCH.values()),
        compiler_params=pltpu.CompilerParams(collective_id=0, has_side_effects=True, vmem_limit_bytes=56 * 2**20),
    )(
        y_root.T,
        root_inverse,
        block_map,
        y_child.reshape(16, 96, 256),
        panel.reshape(2, 768, 256),
        child_inverse.reshape(8, 2, 96, 768),
    )
    def split(both_ref, root_ref, child_ref):
        root_ref[...] = both_ref[:32]
        child_ref[0] = both_ref[32:]

    return pl.pallas_call(
        split,
        out_shape=(jax.ShapeDtypeStruct((32, 256), BF), jax.ShapeDtypeStruct((1, 96, 256), BF)),
        in_specs=[vmem],
        out_specs=(vmem, vmem),
    )(both)


def solution(mesh):
    in_specs = (
        P("col", ("leaf", "row")),
        P(("leaf", "row"), "col"),
        P(),
        P("leaf", "row", None),
        P("leaf", "row", "col"),
        P("leaf", "row", "col"),
    )
    out_specs = (P(("leaf", "row", "col"), None), P("leaf", ("row", "col"), None))
    return jax.shard_map(per_device, mesh=mesh, in_specs=in_specs, out_specs=out_specs, check_vma=False)
```
